32 devices in a mesh: groups: 2 (over y), feat: 4 (over z), trainer: 2 (over x), sub: 2 (over core).
Axes of the slice: x: 2, y: 2, z: 4, core: 2. Of those that a mesh axis runs over, the one named last changes fastest.
Arguments:
- table: bfloat16 [65536, 128], P(('groups', 'feat')), parts along dimension 0, may hold values from -6 to 6
- cur_feats: bfloat16 [81920, 128], P(('groups', 'feat', 'trainer', 'sub')), parts along dimension 0, may hold values from -6 to 6
- nbr_first: int32 [65536, 10], P(('groups', 'feat', 'trainer', 'sub')), parts along dimension 0, may hold values from 0 to 2559
- cnt_first: int32 [65536], P(('groups', 'feat', 'trainer', 'sub')), parts along dimension 0, may hold values from 1 to 10
- nbr_second: int32 [8192, 5], P(('groups', 'feat', 'trainer', 'sub')), parts along dimension 0, may hold values from 0 to 2047
- cnt_second: int32 [8192], P(('groups', 'feat', 'trainer', 'sub')), parts along dimension 0, may hold values from 1 to 5
- w1_self: bfloat16 [256, 256], P('groups'), parts along dimension 0, may hold values from -0.5 to 0.5
- w1_neigh: bfloat16 [256, 256], P('groups'), parts along dimension 0, may hold values from -0.5 to 0.5
- bias_first: float32 [512], P('groups'), parts along dimension 0, may hold values from -3 to 3
- w2_self: bfloat16 [512, 172], P('groups'), parts along dimension 0, may hold values from -0.375 to 0.375
- w2_neigh: bfloat16 [512, 172], P('groups'), parts along dimension 0, may hold values from -0.375 to 0.375
- dlogits: bfloat16 [8192, 172], P(('groups', 'feat', 'trainer', 'sub')), parts along dimension 0, may hold values from -6 to 6
- next_owner: int32 [81920, 1], P(('groups', 'feat', 'trainer', 'sub')), parts along dimension 0, may hold values from 0 to 3; in each aligned block of 2560 rows (0 to 2559, 2560 to 5119, ...) at most 1280 rows name the same one
- next_row: int32 [81920], P(('groups', 'feat', 'trainer', 'sub')), parts along dimension 0, may hold values from 0 to 8191
Outputs:
- next_feats: bfloat16 [81920, 128], P(('groups', 'feat', 'trainer', 'sub')), parts along dimension 0
- grad_w1_self: bfloat16 [256, 256], P(('groups', 'trainer', 'sub')), parts along dimension 0
- grad_w1_neigh: bfloat16 [256, 256], P(('groups', 'trainer', 'sub')), parts along dimension 0
- grad_bias_first: bfloat16 [512], P(('groups', 'trainer', 'sub')), parts along dimension 0
- grad_w2_self: bfloat16 [512, 172], P(('groups', 'trainer', 'sub')), parts along dimension 0
- grad_w2_neigh: bfloat16 [512, 172], P(('groups', 'trainer', 'sub')), parts along dimension 0
The draws below stay inside these ranges and needn't reach their ends.
There are 2 independent parts, one for each index of `groups`. The reference program is written for one: setup_inputs(seed, part) draws one part's arguments, and reference() takes and returns one part's arrays. A program takes and returns all parts, laid end to end along the dimension named above; each array names one. Nothing has to cross between parts.
Inputs may be any that keep to these rules, and one draw needn't show every extreme that they name: `next_owner`: among the 2560 rows of one device, at most 1280 name the same owner, and in every draw some owner is named by exactly 1280 rows of some device. `nbr_first`: indices into the 2560 frontier rows of the same device block. `nbr_second`: indices into the 2048 destinations of the same device block.
All inputs are finite; a program needn't handle non-finite values.
Results may differ from the reference program's by a relative error of at most 0.012.
Values may be sent and summed in bfloat16 or wider, within the bound.
A program may use at most 64 MiB of HBM per device.

```python
import math
import jax
import jax.numpy as jnp
import numpy as np
from jax import lax

D_IN = 128
HID = 256
CLASSES = 172
FAN_A = 10
FAN_B = 5
SEEDS = 256
OWN = 8192
MID = 2048
FRONT = 2560
CAP = 1280
ROWS = 32768
FRONT_ALL = 40960
MID_ALL = 32768
SEEDS_ALL = 4096
N_FEAT = 4
N_TRAINER = 2
N_SUB = 2


def place_ends(entries, stream_key, low, high):
    dims = entries.shape
    index_at = [jax.random.randint(jax.random.fold_in(stream_key, axis), (), 0, dims[axis]) for axis in range(len(dims))]
    entries = entries.at[tuple(index_at)].set(low)
    longest = dims.index(max(dims))
    index_at[longest] = (index_at[longest] + 1) % dims[longest]
    return entries.at[tuple(index_at)].set(high)


def block_levels(own_key, extent, split, low, top_value):
    loudness = 1.0
    for dim, shards_of in split:
        steps = jax.random.uniform(jax.random.fold_in(jax.random.fold_in(own_key, 6), dim), (shards_of,), jnp.float32, low / len(split), top_value / len(split))
        loudness = loudness * jnp.repeat(jnp.exp(steps), extent[dim] // shards_of).reshape((-1,) + (1,) * (len(extent) - 1 - dim))
    return loudness


def assign_block(rng, own, number, rows, number_of, top, limit, skew):
    ranking = jax.random.permutation(rng, number_of)
    heavy_load, ordinary = shares(number_of, rows * top, limit, skew, True), shares(number_of, rows * top, limit, skew, False)
    places = jnp.arange(number_of)

    def named(tallies, rotation):
        used = int((tallies > 0).sum())
        fixed = max(1, used // 4)
        moved = fixed + (places - fixed + rotation * (used - fixed)) % max(1, number_of - fixed)
        return jnp.zeros((number_of,), jnp.int32).at[ranking[jnp.where(places < fixed, places, moved)]].set(jnp.asarray(tallies, jnp.int32))

    tallies = jnp.where(number % 4 == 0, named(heavy_load, number // 4), named(ordinary, number - number // 4 - 1))
    mixed = jax.random.permutation(jax.random.fold_in(own, 3), number_of)
    giver, receiver = mixed[0:number_of // 2 * 2:2], mixed[1:number_of // 2 * 2:2]
    room = jnp.minimum(tallies[giver] - 1, limit - tallies[receiver]) // 2
    room = jnp.where((giver == ranking[0]) | (receiver == ranking[0]) | (tallies[receiver] == 0), 0, jnp.maximum(room, 0))
    moved = jax.random.randint(jax.random.fold_in(own, 4), (number_of // 2,), 0, 1 << 20) % (room + 1)
    tallies = tallies.at[giver].add(-moved).at[receiver].add(moved)
    items = jnp.searchsorted(jnp.cumsum(tallies), jnp.arange(rows * top), side="right").astype(jnp.int32)
    table = items.reshape(top, rows).T
    table = table[jax.random.permutation(jax.random.fold_in(own, 1), rows)]
    rotation = jax.random.randint(jax.random.fold_in(own, 2), (rows, 1), 0, top)
    return jnp.take_along_axis(table, (jnp.arange(top)[None, :] + rotation) % top, axis=1)


def shares(amount, total, reach, slope, full):
    portions = [(1 << 20) // math.isqrt(rank ** slope) + 1 for rank in range(1, amount + 1)]
    largest = reach if full else min(reach, max(-(-total // amount), total * portions[0] // sum(portions)))
    least = 1 if total - largest >= amount - 1 else 0
    holding, rest = [largest] + [least] * (amount - 1), total - largest - least * (amount - 1)
    while rest > 0:
        movable = [i for i in range(1, amount) if holding[i] < largest] or [i for i in range(1, amount) if holding[i] < reach]
        whole, left = sum([portions[i] for i in movable]), rest
        for i in movable:
            addition = min(reach - holding[i], max(1, left * portions[i] // whole), rest)
            holding[i] = holding[i] + addition
            rest = rest - addition
    return np.array(holding)


def bell_draw(rng, shape, spread, most, cuts=(), kind=jnp.bfloat16):
    drawn = spread * jax.random.normal(rng, shape, jnp.float32)
    if cuts:
        drawn = drawn * block_levels(rng, shape, cuts, -0.22, 0.18)
    return jnp.clip(drawn, -most, most).astype(kind)


def setup_inputs(seed: int = 0, part: int = 0) -> dict:
    streams_of = jax.random.split(jax.random.key(seed), 15)
    part_keys = jax.random.split(jax.random.fold_in(streams_of[14], part), 15)
    table = bell_draw(part_keys[0], (ROWS, D_IN), 1.0, 6.0, ((0, 4),))
    cur_feats = bell_draw(part_keys[1], (FRONT_ALL, D_IN), 1.0, 6.0, ((0, 16),))
    nbr_first = place_ends(jax.random.randint(part_keys[2], (MID_ALL, FAN_A), 0, FRONT), jax.random.fold_in(part_keys[2], 1), 0, FRONT - 1).astype(jnp.int32)
    cnt_first = place_ends(jax.random.randint(part_keys[3], (MID_ALL,), 1, FAN_A + 1), jax.random.fold_in(part_keys[3], 1), 1, FAN_A).astype(jnp.int32)
    nbr_second = place_ends(jax.random.randint(part_keys[4], (SEEDS_ALL, FAN_B), 0, MID), jax.random.fold_in(part_keys[4], 1), 0, MID - 1).astype(jnp.int32)
    cnt_second = place_ends(jax.random.randint(part_keys[5], (SEEDS_ALL,), 1, FAN_B + 1), jax.random.fold_in(part_keys[5], 1), 1, FAN_B).astype(jnp.int32)
    w1_self = bell_draw(part_keys[6], (D_IN, HID), D_IN ** -0.5, 0.5)
    w1_neigh = bell_draw(part_keys[7], (D_IN, HID), D_IN ** -0.5, 0.5)
    bias_first = bell_draw(part_keys[8], (HID,), 0.5, 3.0, (), jnp.float32)
    w2_self = bell_draw(part_keys[9], (HID, CLASSES), HID ** -0.5, 0.375)
    w2_neigh = bell_draw(part_keys[10], (HID, CLASSES), HID ** -0.5, 0.375)
    dlogits = bell_draw(part_keys[11], (SEEDS_ALL, CLASSES), 1.0, 6.0, ((0, 16),))
    next_owner_keys = jax.random.split(jax.random.fold_in(part_keys[12], 1), FRONT_ALL // FRONT)
    next_owner_turns = jax.random.permutation(jax.random.fold_in(part_keys[12], 3), FRONT_ALL // FRONT)
    next_owner = jax.vmap(lambda own, number: assign_block(jax.random.fold_in(part_keys[12], 2), own, number, FRONT, N_FEAT, 1, CAP, 2))(next_owner_keys, next_owner_turns).reshape((FRONT_ALL, 1))
    next_row = place_ends(jax.random.randint(part_keys[13], (FRONT_ALL,), 0, OWN), jax.random.fold_in(part_keys[13], 1), 0, OWN - 1).astype(jnp.int32)
    return {"table": table, "cur_feats": cur_feats, "nbr_first": nbr_first, "cnt_first": cnt_first, "nbr_second": nbr_second, "cnt_second": cnt_second, "w1_self": w1_self, "w1_neigh": w1_neigh, "bias_first": bias_first, "w2_self": w2_self, "w2_neigh": w2_neigh, "dlogits": dlogits, "next_owner": next_owner, "next_row": next_row}


def tdot(left, right):
    return lax.dot_general(left, right, (((0,), (0,)), ((), ())), preferred_element_type=jnp.float32)

def mean_rows(source, index, count):
    total = jnp.zeros((index.shape[0], source.shape[1]), jnp.float32)
    for k in range(index.shape[1]):
        picked = source[index[:, k]].astype(jnp.float32)
        total = total + jnp.where((k < count)[:, None], picked, 0.0)
    return (total / count[:, None].astype(jnp.float32)).astype(jnp.bfloat16)

def device_terms(h_zero, nbr_one, cnt_one, nbr_two, cnt_two, grad_out, w1s, w1n, bias, w2s, w2n):
    mid_rows = nbr_one.shape[0]
    seed_rows = nbr_two.shape[0]
    agg_one = mean_rows(h_zero, nbr_one, cnt_one)
    selfrows = h_zero[:mid_rows]
    pre = jnp.dot(selfrows, w1s, preferred_element_type=jnp.float32)
    pre = pre + jnp.dot(agg_one, w1n, preferred_element_type=jnp.float32) + bias
    hidden = jax.nn.silu(pre).astype(jnp.bfloat16)
    agg_two = mean_rows(hidden, nbr_two, cnt_two)
    t2s = tdot(hidden[:seed_rows], grad_out)
    t2n = tdot(agg_two, grad_out)
    dself = lax.dot_general(grad_out, w2s, (((1,), (1,)), ((), ())), preferred_element_type=jnp.float32)
    dneigh = lax.dot_general(grad_out, w2n, (((1,), (1,)), ((), ())), preferred_element_type=jnp.float32)
    dneigh = dneigh / cnt_two[:, None].astype(jnp.float32)
    dhid = jnp.zeros(pre.shape, jnp.float32).at[:seed_rows].add(dself)
    for k in range(nbr_two.shape[1]):
        dhid = dhid.at[nbr_two[:, k]].add(jnp.where((k < cnt_two)[:, None], dneigh, 0.0))
    sig = jax.nn.sigmoid(pre)
    dpre = (dhid * sig * (1.0 + pre * (1.0 - sig))).astype(jnp.bfloat16)
    t1s = tdot(selfrows, dpre)
    t1n = tdot(agg_one, dpre)
    tb1 = lax.optimization_barrier(jnp.sum(dpre.astype(jnp.float32), axis=0))
    return (t1s, t1n, tb1, t2s, t2n)

def reference(table, cur_feats, nbr_first, cnt_first, nbr_second, cnt_second, w1_self, w1_neigh, bias_first, w2_self, w2_neigh, dlogits, next_owner, next_row):
    ndev = N_FEAT * N_TRAINER * N_SUB
    blocks = (cur_feats.reshape(ndev, FRONT, D_IN), nbr_first.reshape(ndev, MID, FAN_A), cnt_first.reshape(ndev, MID), nbr_second.reshape(ndev, SEEDS, FAN_B), cnt_second.reshape(ndev, SEEDS), dlogits.reshape(ndev, SEEDS, CLASSES))

    def accumulate(carry, block):
        terms = device_terms(*block, w1_self, w1_neigh, bias_first, w2_self, w2_neigh)
        return (tuple((a + b for a, b in zip(carry, terms))), None)
    start = (jnp.zeros((D_IN, HID), jnp.float32), jnp.zeros((D_IN, HID), jnp.float32), jnp.zeros((HID,), jnp.float32), jnp.zeros((HID, CLASSES), jnp.float32), jnp.zeros((HID, CLASSES), jnp.float32))
    totals, _ = lax.scan(accumulate, start, blocks)
    factor = 1.0 / jnp.sqrt(jnp.float32(SEEDS * ndev))
    grads = [(t * factor).astype(jnp.bfloat16) for t in totals]
    fetched = table[next_owner[:, 0] * OWN + next_row]
    return (fetched, grads[0], grads[1], grads[2], grads[3], grads[4])
```

```python
import functools

import jax
import jax.numpy as jnp
from jax import lax
from jax.experimental import pallas as pl
from jax.experimental.pallas import tpu as pltpu
from jax.sharding import PartitionSpec as P

BF = jnp.bfloat16
F32 = jnp.float32
VM = pl.BlockSpec(memory_space=pltpu.VMEM)
SM = pl.BlockSpec(memory_space=pltpu.SMEM)
MESH = pl.DeviceIdType.MESH
LANES = 128


def mm(left, right):
    return jnp.dot(left, right, preferred_element_type=F32)


def mm_nt(left, right):
    return lax.dot_general(left, right, (((1,), (1,)), ((), ())), preferred_element_type=F32)


def mm_tn(left, right):
    return lax.dot_general(left, right, (((0,), (0,)), ((), ())), preferred_element_type=F32)


def iota(shape, dim):
    return lax.broadcasted_iota(jnp.int32, shape, dim)


def route_kernel(owners, capacity, owner_ref, row_ref, slot_ref, send_ref, own_pad):
    rows = owner_ref.shape[0]
    padded = own_pad.shape[0]
    own_pad[...] = jnp.full(own_pad.shape, -1, jnp.int32)
    own_pad[0:rows, :] = owner_ref[...]
    own = own_pad[...]
    before = (iota((LANES, LANES), 0) < iota((LANES, LANES), 1)).astype(F32).astype(BF)
    every = jnp.ones((LANES, LANES), BF)
    above = (iota((padded, padded), 0) > iota((padded, padded), 1)).astype(F32).astype(BF)
    rank = jnp.zeros(own.shape, F32)
    for o in range(owners):
        named = (own == o).astype(F32)
        named16 = named.astype(BF)
        inside = mm(named16, before)
        totals = mm(named16, every).astype(BF)
        rank = rank + named * (inside + mm(above, totals))
    slot = own * capacity + rank.astype(jnp.int32)
    slot = slot[0:rows, :]
    slot_ref[...] = slot
    row = row_ref[...]
    high, low = (row >> 6).astype(F32), (row & 63).astype(F32)
    group, place = slot >> 7, slot & 127
    groups = send_ref.shape[0]
    total = jnp.zeros((2 * groups, LANES), F32)
    gid = iota((groups, LANES), 0)
    lid = iota((LANES, LANES), 0)
    for r in range(rows):
        hit = gid == group[r : r + 1, :]
        left = jnp.concatenate(
            [jnp.where(hit, high[r : r + 1, :], 0.0), jnp.where(hit, low[r : r + 1, :], 0.0)], axis=0
        ).astype(BF)
        right = (lid == place[r : r + 1, :]).astype(F32).astype(BF)
        total = total + mm_nt(left, right)
    send_ref[...] = (total[:groups] * 64.0 + total[groups:]).astype(jnp.int32)


def route(owner, row, owners, capacity):
    rows = owner.shape[0] // LANES
    padded = -(-rows // 16) * 16
    groups = owners * capacity // LANES
    return pl.pallas_call(
        functools.partial(route_kernel, owners, capacity),
        out_shape=(
            jax.ShapeDtypeStruct((rows, LANES), jnp.int32),
            jax.ShapeDtypeStruct((groups, LANES), jnp.int32),
        ),
        in_specs=[VM, VM],
        out_specs=(VM, VM),
        scratch_shapes=[pltpu.VMEM((padded, LANES), jnp.int32)],
        name="route",
    )(owner.reshape(rows, LANES), row.reshape(rows, LANES))


def take_kernel(index_ref, source_ref, out_ref, wide, picked):
    wide[...] = source_ref[...].astype(F32)
    chunk = picked.shape[0]

    @pl.loop(0, out_ref.shape[0] // chunk)
    def _(c):
        base = pl.multiple_of(c * chunk, chunk)
        for j in range(chunk):
            picked[j : j + 1, :] = wide[pl.ds(index_ref[base + j], 1), :]
        out_ref[pl.ds(base, chunk), :] = picked[...].astype(BF)


def take(source, index):
    count = index.shape[0]
    width = source.shape[1]
    chunk = 64
    return pl.pallas_call(
        take_kernel,
        out_shape=jax.ShapeDtypeStruct((count, width), BF),
        in_specs=[SM, VM],
        out_specs=VM,
        scratch_shapes=[pltpu.VMEM(source.shape, F32), pltpu.VMEM((chunk, width), F32)],
        compiler_params=pltpu.CompilerParams(vmem_limit_bytes=24 << 20),
        cost_estimate=pl.CostEstimate(flops=0, bytes_accessed=20 << 20, transcendentals=0),
        name="take_rows",
    )(index, source)


def train_kernel(
    copies,
    feats_t_ref,
    nbr1_ref,
    cnt1_ref,
    nbr2_ref,
    cnt2_ref,
    w1s_ref,
    w1n_ref,
    bias_ref,
    w2s_ref,
    w2n_ref,
    dlog_ref,
    out_ref,
    counts1,
    counts2,
    agg_t,
    z_t,
    hid_t,
):
    width, front = feats_t_ref.shape
    fan1, mid = nbr1_ref.shape
    fan2, seeds = nbr2_ref.shape
    hidden, classes = w2s_ref.shape
    chunk = seeds
    w1s_t, w1n_t = w1s_ref[...].T, w1n_ref[...].T
    bias = bias_ref[...]
    strip = 32
    one, zero = jnp.ones((strip, chunk), BF), jnp.zeros((strip, chunk), BF)
    base_row = iota((strip, chunk), 0).astype(F32)

    def strips(index_rows, valid_rows, length, put):
        for block in range(0, length, 256):
            rel = []
            for idx, ok in zip(index_rows, valid_rows):
                off = idx - block
                off = jnp.where(ok & (off >= 0) & (off < 256), off, -1).astype(F32)
                rel.append(jnp.broadcast_to(off, (strip, chunk)).astype(BF))
            for s in range(0, min(256, length - block), strip):
                rows = (base_row + float(s)).astype(BF)
                acc = jnp.where(rel[0] == rows, one, zero)
                for r in rel[1:]:
                    acc = acc + jnp.where(r == rows, one, zero)
                put(block + s, acc)

    cnt2 = cnt2_ref[...]

    def put2(at, value):
        counts2[at : at + strip, :] = value

    strips(
        [nbr2_ref[k : k + 1, :] for k in range(fan2)],
        [cnt2 > k for k in range(fan2)],
        mid,
        put2,
    )

    def put1(at, value):
        counts1[at : at + strip, :] = value

    @pl.loop(0, mid // chunk)
    def _(c):
        at = pl.ds(pl.multiple_of(c * chunk, chunk), chunk)
        cnt = cnt1_ref[:, at]
        strips([nbr1_ref[k : k + 1, at] for k in range(fan1)], [cnt > k for k in range(fan1)], front, put1)
        agg = (mm(feats_t_ref[...], counts1[...]) / cnt.astype(F32)).astype(BF)
        agg_t[:, at] = agg
        z = mm(w1s_t, feats_t_ref[:, at]) + mm(w1n_t, agg) + bias
        z_t[:, at] = z
        hid_t[:, at] = (z * jax.nn.sigmoid(z)).astype(BF)

    dlog = dlog_ref[...]
    cnt2f = cnt2.astype(F32)
    agg2_t = (mm(hid_t[...], counts2[...]) / cnt2f).astype(BF)
    t2s = mm(hid_t[:, 0:seeds], dlog)
    t2n = mm(agg2_t, dlog)
    dself_t = mm_nt(w2s_ref[...], dlog)
    dneigh_t = mm_nt(w2n_ref[...], dlog) / cnt2f
    dn_high = dneigh_t.astype(BF)
    dn_low = (dneigh_t - dn_high.astype(F32)).astype(BF)
    t1s = jnp.zeros((width, hidden), F32)
    t1n = jnp.zeros((width, hidden), F32)
    tb1 = jnp.zeros((16, hidden), F32)
    ones = jnp.ones((16, chunk), BF)
    for c in range(0, mid, chunk):
        part = counts2[c : c + chunk, :]
        dh = mm_nt(dn_high, part) + mm_nt(dn_low, part)
        if c == 0:
            dh = dh + dself_t
        z = z_t[:, c : c + chunk]
        sig = jax.nn.sigmoid(z)
        dz = (dh * sig * (1.0 + z * (1.0 - sig))).astype(BF)
        t1s = t1s + mm_nt(feats_t_ref[:, c : c + chunk], dz)
        t1n = t1n + mm_nt(agg_t[:, c : c + chunk], dz)
        tb1 = tb1 + mm_nt(ones, dz)
    r1, r2 = width // copies, hidden // copies
    for p in range(copies):
        out_ref[p, 0:r1, :] = t1s[p * r1 : (p + 1) * r1].astype(BF)
        out_ref[p, r1 : 2 * r1, :] = t1n[p * r1 : (p + 1) * r1].astype(BF)
        two = 2 * r1
        out_ref[p, two : two + 2 * r2, :] = jnp.zeros((2 * r2, hidden), BF)
        out_ref[p, two : two + r2, 0:classes] = t2s[p * r2 : (p + 1) * r2].astype(BF)
        out_ref[p, two + r2 : two + 2 * r2, 0:classes] = t2n[p * r2 : (p + 1) * r2].astype(BF)
        out_ref[p, two + 2 * r2 :, :] = tb1.astype(BF)


def train(copies, feats, nbr1, cnt1, nbr2, cnt2, w1s, w1n, bias, w2s, w2n, dlog):
    front, width = feats.shape
    mid, seeds = nbr1.shape[0], nbr2.shape[0]
    hidden = w1s.shape[1]
    rows = 2 * width // copies + 2 * hidden // copies + 16
    return pl.pallas_call(
        functools.partial(train_kernel, copies),
        out_shape=jax.ShapeDtypeStruct((copies, rows, hidden), BF),
        in_specs=[VM] * 11,
        out_specs=VM,
        scratch_shapes=[
            pltpu.VMEM((front, seeds), BF),
            pltpu.VMEM((mid, seeds), BF),
            pltpu.VMEM((width, mid), BF),
            pltpu.VMEM((hidden, mid), F32),
            pltpu.VMEM((hidden, mid), BF),
        ],
        compiler_params=pltpu.CompilerParams(vmem_limit_bytes=32 << 20),
        cost_estimate=pl.CostEstimate(flops=4 << 30, bytes_accessed=60 << 20, transcendentals=1 << 20),
        name="train",
    )(feats.T, nbr1.T, cnt1[None, :], nbr2.T, cnt2[None, :], w1s, w1n, bias[:, None], w2s, w2n, dlog)


def reduce_kernel(owners, trainers, subs, factor, in_ref, out_ref, got, part, fed, s1, r1, s2, r2):
    copies = trainers * subs
    me = lax.axis_index("trainer") * subs + lax.axis_index("sub")
    feat = lax.axis_index("feat")

    def peer(d):
        p = lax.rem(me + d, copies)
        return p, {"trainer": p // subs, "sub": lax.rem(p, subs)}

    barrier = pltpu.get_barrier_semaphore()
    for d in range(1, copies):
        pl.semaphore_signal(barrier, inc=1, device_id=peer(d)[1], device_id_type=MESH)
    for d in range(1, owners):
        pl.semaphore_signal(
            barrier, inc=1, device_id={"feat": lax.rem(feat + d, owners)}, device_id_type=MESH
        )
    pl.semaphore_wait(barrier, copies + owners - 2)
    first = []
    for d in range(1, copies):
        p, where = peer(d)
        copy = pltpu.make_async_remote_copy(
            src_ref=in_ref.at[p],
            dst_ref=got.at[d - 1],
            send_sem=s1.at[d - 1],
            recv_sem=r1.at[d - 1],
            device_id=where,
            device_id_type=MESH,
        )
        copy.start()
        first.append(copy)
    total = in_ref[me].astype(F32)
    for d in range(1, copies):
        first[d - 1].wait_recv()
        total = total + got[d - 1].astype(F32)
    part[...] = total.astype(BF)
    second = []
    for d in range(1, owners):
        copy = pltpu.make_async_remote_copy(
            src_ref=part,
            dst_ref=fed.at[feat],
            send_sem=s2.at[d - 1],
            recv_sem=r2.at[d - 1],
            device_id={"feat": lax.rem(feat + d, owners)},
            device_id_type=MESH,
        )
        copy.start()
        second.append(copy)
    fed[feat] = part[...]
    for copy in second:
        copy.wait_recv()
    total = fed[0].astype(F32)
    for f in range(1, owners):
        total = total + fed[f].astype(F32)
    out_ref[...] = (total * factor).astype(BF)
    for copy in first + second:
        copy.wait_send()


def reduce_grads(packed, owners, trainers, subs, factor):
    copies, rows, hidden = packed.shape
    return pl.pallas_call(
        functools.partial(reduce_kernel, owners, trainers, subs, factor),
        out_shape=jax.ShapeDtypeStruct((rows, hidden), BF),
        in_specs=[VM],
        out_specs=VM,
        scratch_shapes=[
            pltpu.VMEM((copies - 1, rows, hidden), BF),
            pltpu.VMEM((rows, hidden), BF),
            pltpu.VMEM((owners, rows, hidden), BF),
            pltpu.SemaphoreType.DMA((copies - 1,)),
            pltpu.SemaphoreType.DMA((copies - 1,)),
            pltpu.SemaphoreType.DMA((owners - 1,)),
            pltpu.SemaphoreType.DMA((owners - 1,)),
        ],
        compiler_params=pltpu.CompilerParams(
            collective_id=0, has_side_effects=True, vmem_limit_bytes=24 << 20
        ),
        cost_estimate=pl.CostEstimate(flops=0, bytes_accessed=40 << 20, transcendentals=0),
        name="reduce_grads",
    )(packed)


def shards(
    trainers,
    subs,
    owners,
    table,
    cur_feats,
    nbr_first,
    cnt_first,
    nbr_second,
    cnt_second,
    w1_self,
    w1_neigh,
    bias_first,
    w2_self,
    w2_neigh,
    dlogits,
    next_owner,
    next_row,
):
    copies = trainers * subs
    front_rows, width = cur_feats.shape
    hidden, classes = w2_self.shape
    capacity = 2 * front_rows // owners
    slot, send = route(next_owner[:, 0], next_row, owners, capacity)
    asked = lax.all_to_all(
        send.reshape(owners, capacity), "feat", split_axis=0, concat_axis=0, tiled=True
    )
    found = take(table, asked.reshape(-1)).reshape(owners, capacity, width)
    replies = lax.all_to_all(found, "feat", split_axis=0, concat_axis=0, tiled=True)
    packed = train(
        copies,
        cur_feats,
        nbr_first,
        cnt_first,
        nbr_second,
        cnt_second,
        w1_self,
        w1_neigh,
        bias_first,
        w2_self,
        w2_neigh,
        dlogits,
    )
    seeds_all = nbr_second.shape[0] * owners * copies
    summed = reduce_grads(packed, owners, trainers, subs, float(seeds_all) ** -0.5)
    next_feats = take(replies.reshape(-1, width), slot.reshape(-1))
    r1, r2 = width // copies, hidden // copies
    two = 2 * r1
    me = lax.axis_index("trainer") * subs + lax.axis_index("sub")
    return (
        next_feats,
        summed[0:r1],
        summed[r1:two],
        lax.dynamic_slice(summed[two + 2 * r2], (me * r2,), (r2,)),
        summed[two : two + r2, 0:classes],
        summed[two + r2 : two + 2 * r2, 0:classes],
    )


def solution(mesh):
    every = ("groups", "feat", "trainer", "sub")
    share = ("groups", "trainer", "sub")
    placed = (
        P(("groups", "feat"), None),
        P(every, None),
        P(every, None),
        P(every),
        P(every, None),
        P(every),
        P("groups", None),
        P("groups", None),
        P("groups"),
        P("groups", None),
        P("groups", None),
        P(every, None),
        P(every, None),
        P(every),
    )
    shape = mesh.shape
    return jax.shard_map(
        functools.partial(shards, shape["trainer"], shape["sub"], shape["feat"]),
        mesh=mesh,
        in_specs=placed,
        out_specs=(
            P(every, None),
            P(share, None),
            P(share, None),
            P(share),
            P(share, None),
            P(share, None),
        ),
        check_vma=False,
    )
```

```python
import functools

import jax
import jax.numpy as jnp
from jax import lax
from jax.experimental import pallas as pl
from jax.experimental.pallas import tpu as pltpu
from jax.sharding import PartitionSpec as P

BF = jnp.bfloat16
F32 = jnp.float32
VM = pl.BlockSpec(memory_space=pltpu.VMEM)
SM = pl.BlockSpec(memory_space=pltpu.SMEM)
MESH = pl.DeviceIdType.MESH
LANES = 128


def mm(left, right):
    return jnp.dot(left, right, preferred_element_type=F32)


def mm_nt(left, right):
    return lax.dot_general(left, right, (((1,), (1,)), ((), ())), preferred_element_type=F32)


def mm_tn(left, right):
    return lax.dot_general(left, right, (((0,), (0,)), ((), ())), preferred_element_type=F32)


def iota(shape, dim):
    return lax.broadcasted_iota(jnp.int32, shape, dim)


def make_requests(owners, capacity, owner_ref, row_ref, slot_ref, send_ref, own_pad):
    rows = owner_ref.shape[0]
    padded = own_pad.shape[0]
    own_pad[...] = jnp.full(own_pad.shape, -1, jnp.int32)
    own_pad[0:rows, :] = owner_ref[...]
    own = own_pad[...]
    before = (iota((LANES, LANES), 0) < iota((LANES, LANES), 1)).astype(F32).astype(BF)
    every = jnp.ones((LANES, LANES), BF)
    above = (iota((padded, padded), 0) > iota((padded, padded), 1)).astype(F32).astype(BF)
    rank = jnp.zeros(own.shape, F32)
    for o in range(owners):
        named = (own == o).astype(F32)
        named16 = named.astype(BF)
        inside = mm(named16, before)
        totals = mm(named16, every).astype(BF)
        rank = rank + named * (inside + mm(above, totals))
    slot = own * capacity + rank.astype(jnp.int32)
    slot = slot[0:rows, :]
    slot_ref[...] = slot
    row = row_ref[...]
    high, low = (row >> 6).astype(F32), (row & 63).astype(F32)
    group, place = slot >> 7, slot & 127
    each = capacity // LANES
    groups = owners * each
    total = jnp.zeros((2 * groups, LANES), F32)
    gid = iota((groups, LANES), 0)
    lid = iota((LANES, LANES), 0)
    for r in range(rows):
        hit = gid == group[r : r + 1, :]
        left = jnp.concatenate(
            [jnp.where(hit, high[r : r + 1, :], 0.0), jnp.where(hit, low[r : r + 1, :], 0.0)], axis=0
        ).astype(BF)
        right = (lid == place[r : r + 1, :]).astype(F32).astype(BF)
        total = total + mm_nt(left, right)
    asked = (total[:groups] * 64.0 + total[groups:]).astype(jnp.int32)
    send_ref[...] = jnp.zeros(send_ref.shape, jnp.int32)
    for o in range(owners):
        send_ref[o, 0:each, :] = asked[o * each : (o + 1) * each]


def step_kernel(
    owners,
    trainers,
    subs,
    capacity,
    factor,
    owner_ref,
    row_ref,
    table_ref,
    feats_t_ref,
    nbr1_ref,
    cnt1_ref,
    nbr2_ref,
    cnt2_ref,
    w1s_ref,
    w1n_ref,
    bias_ref,
    w2s_ref,
    w2n_ref,
    dlog_ref,
    slot_ref,
    replies_ref,
    out_ref,
    own_pad,
    send,
    asked,
    asked_s,
    wide,
    picked,
    found,
    counts1,
    counts2,
    agg_t,
    z_t,
    hid_t,
    packed,
    got,
    part,
    fed,
    load_sem,
    ask_s,
    ask_r,
    rep_s,
    rep_r,
    s1,
    r1,
    s2,
    r2,
):
    copies = trainers * subs
    me = lax.axis_index("trainer") * subs + lax.axis_index("sub")
    feat = lax.axis_index("feat")

    def peer(d):
        p = lax.rem(me + d, copies)
        return p, {"trainer": p // subs, "sub": lax.rem(p, subs)}

    def remote(src, dst, send_sem, recv_sem, where):
        copy = pltpu.make_async_remote_copy(
            src_ref=src,
            dst_ref=dst,
            send_sem=send_sem,
            recv_sem=recv_sem,
            device_id=where,
            device_id_type=MESH,
        )
        copy.start()
        return copy

    barrier = pltpu.get_barrier_semaphore()
    for d in range(1, copies):
        pl.semaphore_signal(barrier, inc=1, device_id=peer(d)[1], device_id_type=MESH)
    for d in range(1, owners):
        pl.semaphore_signal(
            barrier, inc=1, device_id={"feat": lax.rem(feat + d, owners)}, device_id_type=MESH
        )
    make_requests(owners, capacity, owner_ref, row_ref, slot_ref, send, own_pad)
    pl.semaphore_wait(barrier, copies + owners - 2)
    order = sorted(range(1, owners), key=lambda d: abs(2 * d - owners))
    asks = []
    for d in order:
        to = lax.rem(feat + d, owners)
        asks.append(
            remote(send.at[to], asked.at[feat], ask_s.at[d - 1], ask_r.at[d - 1], {"feat": to})
        )
    asked[feat] = send[feat]
    wide[...] = table_ref[...].astype(F32)

    width, front = feats_t_ref.shape
    fan1, mid = nbr1_ref.shape
    fan2, seeds = nbr2_ref.shape
    hidden, classes = w2s_ref.shape
    chunk = seeds
    w1s_t, w1n_t = w1s_ref[...].T, w1n_ref[...].T
    bias = bias_ref[...]
    strip = 32
    one, zero = jnp.ones((strip, chunk), BF), jnp.zeros((strip, chunk), BF)
    base_row = iota((strip, chunk), 0).astype(F32)

    def strips(index_rows, valid_rows, length, put):
        for block in range(0, length, 256):
            rel = []
            for idx, ok in zip(index_rows, valid_rows):
                off = idx - block
                off = jnp.where(ok & (off >= 0) & (off < 256), off, -1).astype(F32)
                rel.append(jnp.broadcast_to(off, (strip, chunk)).astype(BF))
            for s in range(0, min(256, length - block), strip):
                rows = (base_row + float(s)).astype(BF)
                acc = jnp.where(rel[0] == rows, one, zero)
                for r in rel[1:]:
                    acc = acc + jnp.where(r == rows, one, zero)
                put(block + s, acc)

    cnt2 = cnt2_ref[...]

    def put2(at, value):
        counts2[at : at + strip, :] = value

    strips(
        [nbr2_ref[k : k + 1, :] for k in range(fan2)],
        [cnt2 > k for k in range(fan2)],
        mid,
        put2,
    )

    def put1(at, value):
        counts1[at : at + strip, :] = value

    def first_layer(c):
        at = pl.ds(pl.multiple_of(c * chunk, chunk), chunk)
        cnt = cnt1_ref[:, at]
        strips([nbr1_ref[k : k + 1, at] for k in range(fan1)], [cnt > k for k in range(fan1)], front, put1)
        agg = (mm(feats_t_ref[...], counts1[...]) / cnt.astype(F32)).astype(BF)
        agg_t[:, at] = agg
        z = mm(w1s_t, feats_t_ref[:, at]) + mm(w1n_t, agg) + bias
        z_t[:, at] = z
        hid_t[:, at] = (z * jax.nn.sigmoid(z)).astype(BF)

    @pl.loop(0, 1)
    def _(c):
        first_layer(c)

    for copy in asks:
        copy.wait_recv()
    asked[...] = jnp.clip(asked[...], 0, table_ref.shape[0] - 1)
    load = pltpu.make_async_copy(asked, asked_s, load_sem)
    load.start()
    load.wait()

    def gather(to, target):
        @pl.loop(0, capacity // LANES)
        def _(g):
            for j in range(LANES):
                picked[j : j + 1, :] = wide[pl.ds(asked_s[to, g, j], 1), :]
            target[to, pl.ds(pl.multiple_of(g * LANES, LANES), LANES), :] = picked[...].astype(BF)

    answers = []
    for d in order:
        to = lax.rem(feat + d, owners)
        gather(to, found)
        answers.append(
            remote(found.at[to], replies_ref.at[feat], rep_s.at[d - 1], rep_r.at[d - 1], {"feat": to})
        )
    gather(feat, replies_ref)

    @pl.loop(1, mid // chunk)
    def _(c):
        first_layer(c)

    dlog = dlog_ref[...]
    cnt2f = cnt2.astype(F32)
    agg2_t = (mm(hid_t[...], counts2[...]) / cnt2f).astype(BF)
    t2s = mm(hid_t[:, 0:seeds], dlog)
    t2n = mm(agg2_t, dlog)
    dself_t = mm_nt(w2s_ref[...], dlog)
    dneigh_t = mm_nt(w2n_ref[...], dlog) / cnt2f
    dn_high = dneigh_t.astype(BF)
    dn_low = (dneigh_t - dn_high.astype(F32)).astype(BF)
    t1s = jnp.zeros((width, hidden), F32)
    t1n = jnp.zeros((width, hidden), F32)
    tb1 = jnp.zeros((16, hidden), F32)
    ones = jnp.ones((16, chunk), BF)
    for c in range(0, mid, chunk):
        block = counts2[c : c + chunk, :]
        dh = mm_nt(dn_high, block) + mm_nt(dn_low, block)
        if c == 0:
            dh = dh + dself_t
        z = z_t[:, c : c + chunk]
        sig = jax.nn.sigmoid(z)
        dz = (dh * sig * (1.0 + z * (1.0 - sig))).astype(BF)
        t1s = t1s + mm_nt(feats_t_ref[:, c : c + chunk], dz)
        t1n = t1n + mm_nt(agg_t[:, c : c + chunk], dz)
        tb1 = tb1 + mm_nt(ones, dz)
    n1, n2 = width // copies, hidden // copies
    for p in range(copies):
        packed[p, 0:n1, :] = t1s[p * n1 : (p + 1) * n1].astype(BF)
        packed[p, n1 : 2 * n1, :] = t1n[p * n1 : (p + 1) * n1].astype(BF)
        two = 2 * n1
        packed[p, two : two + 2 * n2, :] = jnp.zeros((2 * n2, hidden), BF)
        packed[p, two : two + n2, 0:classes] = t2s[p * n2 : (p + 1) * n2].astype(BF)
        packed[p, two + n2 : two + 2 * n2, 0:classes] = t2n[p * n2 : (p + 1) * n2].astype(BF)
        packed[p, two + 2 * n2 :, :] = jnp.zeros((16, hidden), BF)
        packed[p, two + 2 * n2 :, 0:n2] = tb1[:, p * n2 : (p + 1) * n2].astype(BF)
    first = []
    for d in range(1, copies):
        p, where = peer(d)
        first.append(remote(packed.at[p], got.at[d - 1], s1.at[d - 1], r1.at[d - 1], where))
    total = packed[me].astype(F32)
    for d in range(1, copies):
        first[d - 1].wait_recv()
        total = total + got[d - 1].astype(F32)
    part[...] = total.astype(BF)
    second = []
    for d in order:
        second.append(
            remote(part, fed.at[feat], s2.at[d - 1], r2.at[d - 1], {"feat": lax.rem(feat + d, owners)})
        )
    fed[feat] = part[...]
    for copy in second:
        copy.wait_recv()
    total = fed[0].astype(F32)
    for f in range(1, owners):
        total = total + fed[f].astype(F32)
    out_ref[...] = (total * factor).astype(BF)
    for copy in asks + first + second + answers:
        copy.wait_send()
    for copy in answers:
        copy.wait_recv()


def run_step(owners, trainers, subs, capacity, factor, owner, row, table, feats, nbr1, cnt1, nbr2, cnt2, weights, dlog):
    w1s, w1n, bias, w2s, w2n = weights
    copies = trainers * subs
    front, width = feats.shape
    mid, seeds = nbr1.shape[0], nbr2.shape[0]
    hidden = w1s.shape[1]
    lines = front // LANES
    pages = -(-(capacity // LANES) // 8) * 8
    rows = 2 * width // copies + 2 * hidden // copies + 16
    dma = pltpu.SemaphoreType.DMA
    return pl.pallas_call(
        functools.partial(step_kernel, owners, trainers, subs, capacity, factor),
        out_shape=(
            jax.ShapeDtypeStruct((lines, LANES), jnp.int32),
            jax.ShapeDtypeStruct((owners, capacity, width), BF),
            jax.ShapeDtypeStruct((rows, hidden), BF),
        ),
        in_specs=[VM] * 14,
        out_specs=(VM, VM, VM),
        scratch_shapes=[
            pltpu.VMEM((-(-lines // 16) * 16, LANES), jnp.int32),
            pltpu.VMEM((owners, pages, LANES), jnp.int32),
            pltpu.VMEM((owners, pages, LANES), jnp.int32),
            pltpu.SMEM((owners, pages, LANES), jnp.int32),
            pltpu.VMEM(table.shape, F32),
            pltpu.VMEM((LANES, width), F32),
            pltpu.VMEM((owners, capacity, width), BF),
            pltpu.VMEM((front, seeds), BF),
            pltpu.VMEM((mid, seeds), BF),
            pltpu.VMEM((width, mid), BF),
            pltpu.VMEM((hidden, mid), F32),
            pltpu.VMEM((hidden, mid), BF),
            pltpu.VMEM((copies, rows, hidden), BF),
            pltpu.VMEM((copies - 1, rows, hidden), BF),
            pltpu.VMEM((rows, hidden), BF),
            pltpu.VMEM((owners, rows, hidden), BF),
            dma,
            dma((owners - 1,)),
            dma((owners - 1,)),
            dma((owners - 1,)),
            dma((owners - 1,)),
            dma((copies - 1,)),
            dma((copies - 1,)),
            dma((owners - 1,)),
            dma((owners - 1,)),
        ],
        compiler_params=pltpu.CompilerParams(
            collective_id=0, has_side_effects=True, vmem_limit_bytes=40 << 20
        ),
        cost_estimate=pl.CostEstimate(flops=4 << 30, bytes_accessed=60 << 20, transcendentals=1 << 20),
        name="step",
    )(
        owner.reshape(lines, LANES),
        row.reshape(lines, LANES),
        table,
        feats.T,
        nbr1.T,
        cnt1[None, :],
        nbr2.T,
        cnt2[None, :],
        w1s,
        w1n,
        bias[:, None],
        w2s,
        w2n,
        dlog,
    )


def finish_kernel(slot_ref, source_ref, grads_ref, feats_ref, g1s, g1n, gb, g2s, g2n, wide, picked):
    wide[...] = source_ref[...].astype(F32)

    @pl.loop(0, slot_ref.shape[0])
    def _(g):
        for j in range(LANES):
            picked[j : j + 1, :] = wide[pl.ds(slot_ref[g, j], 1), :]
        feats_ref[pl.ds(pl.multiple_of(g * LANES, LANES), LANES), :] = picked[...].astype(BF)

    n1, n2, classes = g1s.shape[0], g2s.shape[0], g2s.shape[1]
    two = 2 * n1
    g1s[...] = grads_ref[0:n1, :]
    g1n[...] = grads_ref[n1:two, :]
    g2s[...] = grads_ref[two : two + n2, 0:classes]
    g2n[...] = grads_ref[two + n2 : two + 2 * n2, 0:classes]
    gb[...] = grads_ref[two + 2 * n2 : two + 2 * n2 + 1, 0:n2]


def finish(slot, replies, grads, n1, n2, classes):
    count = slot.shape[0] * LANES
    width, hidden = replies.shape[1], grads.shape[1]
    return pl.pallas_call(
        finish_kernel,
        out_shape=(
            jax.ShapeDtypeStruct((count, width), BF),
            jax.ShapeDtypeStruct((n1, hidden), BF),
            jax.ShapeDtypeStruct((n1, hidden), BF),
            jax.ShapeDtypeStruct((1, n2), BF),
            jax.ShapeDtypeStruct((n2, classes), BF),
            jax.ShapeDtypeStruct((n2, classes), BF),
        ),
        in_specs=[SM, VM, VM],
        out_specs=(VM,) * 6,
        scratch_shapes=[pltpu.VMEM(replies.shape, F32), pltpu.VMEM((LANES, width), F32)],
        compiler_params=pltpu.CompilerParams(vmem_limit_bytes=24 << 20),
        name="finish",
    )(slot, replies, grads)


def shards(
    trainers,
    subs,
    owners,
    table,
    cur_feats,
    nbr_first,
    cnt_first,
    nbr_second,
    cnt_second,
    w1_self,
    w1_neigh,
    bias_first,
    w2_self,
    w2_neigh,
    dlogits,
    next_owner,
    next_row,
):
    copies = trainers * subs
    front_rows, width = cur_feats.shape
    hidden, classes = w2_self.shape
    capacity = -(-(2 * front_rows // owners) // LANES) * LANES
    seeds_all = nbr_second.shape[0] * owners * copies
    slot, replies, grads = run_step(
        owners,
        trainers,
        subs,
        capacity,
        float(seeds_all) ** -0.5,
        next_owner[:, 0],
        next_row,
        table,
        cur_feats,
        nbr_first,
        cnt_first,
        nbr_second,
        cnt_second,
        (w1_self, w1_neigh, bias_first, w2_self, w2_neigh),
        dlogits,
    )
    n1, n2 = width // copies, hidden // copies
    feats, g1s, g1n, gb, g2s, g2n = finish(
        slot, replies.reshape(-1, width), grads, n1, n2, classes
    )
    return feats, g1s, g1n, gb.reshape(-1), g2s, g2n


def solution(mesh):
    every = ("groups", "feat", "trainer", "sub")
    share = ("groups", "trainer", "sub")
    placed = (
        P(("groups", "feat"), None),
        P(every, None),
        P(every, None),
        P(every),
        P(every, None),
        P(every),
        P("groups", None),
        P("groups", None),
        P("groups"),
        P("groups", None),
        P("groups", None),
        P(every, None),
        P(every, None),
        P(every),
    )
    shape = mesh.shape
    return jax.shard_map(
        functools.partial(shards, shape["trainer"], shape["sub"], shape["feat"]),
        mesh=mesh,
        in_specs=placed,
        out_specs=(
            P(every, None),
            P(share, None),
            P(share, None),
            P(share),
            P(share, None),
            P(share, None),
        ),
        check_vma=False,
    )
```

```python
import functools

import jax
import jax.numpy as jnp
from jax import lax
from jax.experimental import pallas as pl
from jax.experimental.pallas import tpu as pltpu
from jax.sharding import PartitionSpec as P

BF = jnp.bfloat16
F32 = jnp.float32
VM = pl.BlockSpec(memory_space=pltpu.VMEM)
AN = pl.BlockSpec(memory_space=pl.ANY)
SM = pl.BlockSpec(memory_space=pltpu.SMEM)
MESH = pl.DeviceIdType.MESH
LANES = 128


def mm(left, right):
    return jnp.dot(left, right, preferred_element_type=F32)


def mm_nt(left, right):
    return lax.dot_general(left, right, (((1,), (1,)), ((), ())), preferred_element_type=F32)


def mm_tn(left, right):
    return lax.dot_general(left, right, (((0,), (0,)), ((), ())), preferred_element_type=F32)


def iota(shape, dim):
    return lax.broadcasted_iota(jnp.int32, shape, dim)


def make_requests(owners, capacity, owner_ref, row_ref, slot_ref, send_ref, own_pad):
    rows = row_ref.shape[0]
    padded = own_pad.shape[0]
    own_pad[...] = jnp.full(own_pad.shape, -1, jnp.int32)
    for r in range(rows):
        own_pad[r : r + 1, :] = owner_ref[:, r * LANES : (r + 1) * LANES]
    own = own_pad[...]
    before = (iota((LANES, LANES), 0) < iota((LANES, LANES), 1)).astype(F32).astype(BF)
    every = jnp.ones((LANES, LANES), BF)
    above = (iota((padded, padded), 0) > iota((padded, padded), 1)).astype(F32).astype(BF)
    rank = jnp.zeros(own.shape, F32)
    for o in range(owners):
        named = (own == o).astype(F32)
        named16 = named.astype(BF)
        inside = mm(named16, before)
        totals = mm(named16, every).astype(BF)
        rank = rank + named * (inside + mm(above, totals))
    slot = own * capacity + rank.astype(jnp.int32)
    slot = slot[0:rows, :]
    slot_ref[...] = slot
    row = row_ref[...]
    high, low = (row >> 6).astype(F32), (row & 63).astype(F32)
    group, place = slot >> 7, slot & 127
    each = capacity // LANES
    groups = owners * each
    total = jnp.zeros((2 * groups, LANES), F32)
    gid = iota((groups, LANES), 0)
    lid = iota((LANES, LANES), 0)
    for r in range(rows):
        hit = gid == group[r : r + 1, :]
        left = jnp.concatenate(
            [jnp.where(hit, high[r : r + 1, :], 0.0), jnp.where(hit, low[r : r + 1, :], 0.0)], axis=0
        ).astype(BF)
        right = (lid == place[r : r + 1, :]).astype(F32).astype(BF)
        total = total + mm_nt(left, right)
    asked = (total[:groups] * 64.0 + total[groups:]).astype(jnp.int32)
    send_ref[...] = jnp.zeros(send_ref.shape, jnp.int32)
    for o in range(owners):
        send_ref[o, 0:each, :] = asked[o * each : (o + 1) * each]


def step_kernel(
    owners,
    trainers,
    subs,
    capacity,
    factor,
    owner_ref,
    row_ref,
    table_h,
    feats_h,
    nbr1_h,
    cnt1_ref,
    nbr2_ref,
    cnt2_ref,
    w1s_h,
    w1n_h,
    bias_ref,
    w2s_ref,
    w2n_ref,
    dlog_ref,
    slot_ref,
    replies_ref,
    out_ref,
    table_ref,
    feats_v,
    feats_t_ref,
    nbr1_ref,
    w1s_ref,
    w1n_ref,
    fetch_sem,
    own_pad,
    send,
    asked,
    asked_s,
    wide,
    picked,
    found,
    counts1,
    counts2,
    agg_t,
    z_t,
    hid_t,
    packed,
    got,
    part,
    fed,
    load_sem,
    ask_s,
    ask_r,
    rep_s,
    rep_r,
    s1,
    r1,
    s2,
    r2,
):
    copies = trainers * subs
    me = lax.axis_index("trainer") * subs + lax.axis_index("sub")
    feat = lax.axis_index("feat")

    def peer(d):
        p = lax.rem(me + d, copies)
        return p, {"trainer": p // subs, "sub": lax.rem(p, subs)}

    def remote(src, dst, send_sem, recv_sem, where):
        copy = pltpu.make_async_remote_copy(
            src_ref=src,
            dst_ref=dst,
            send_sem=send_sem,
            recv_sem=recv_sem,
            device_id=where,
            device_id_type=MESH,
        )
        copy.start()
        return copy

    fetches = []
    for n, (src, dst) in enumerate(
        (
            (table_h, table_ref),
            (feats_h, feats_v),
            (nbr1_h, nbr1_ref),
            (w1s_h, w1s_ref),
            (w1n_h, w1n_ref),
        )
    ):
        fetches.append(pltpu.make_async_copy(src, dst, fetch_sem.at[n]))
        fetches[-1].start()
    barrier = pltpu.get_barrier_semaphore()
    for d in range(1, copies):
        pl.semaphore_signal(barrier, inc=1, device_id=peer(d)[1], device_id_type=MESH)
    for d in range(1, owners):
        pl.semaphore_signal(
            barrier, inc=1, device_id={"feat": lax.rem(feat + d, owners)}, device_id_type=MESH
        )
    make_requests(owners, capacity, owner_ref, row_ref, slot_ref, send, own_pad)
    pl.semaphore_wait(barrier, copies + owners - 2)
    order = sorted(range(1, owners), key=lambda d: abs(2 * d - owners))
    asks = []
    for d in order:
        to = lax.rem(feat + d, owners)
        asks.append(
            remote(send.at[to], asked.at[feat], ask_s.at[d - 1], ask_r.at[d - 1], {"feat": to})
        )
    asked[feat] = send[feat]
    for fetch in fetches:
        fetch.wait()
    wide[...] = table_ref[...].astype(F32)
    for r in range(0, feats_v.shape[0], LANES):
        feats_t_ref[:, r : r + LANES] = feats_v[r : r + LANES, :].T

    width, front = feats_t_ref.shape
    fan1, mid = nbr1_ref.shape
    fan2, seeds = nbr2_ref.shape
    classes, hidden = w2s_ref.shape
    chunk = seeds
    w1s_t, w1n_t = w1s_ref[...].T, w1n_ref[...].T
    bias = jnp.broadcast_to(bias_ref[...], (LANES, hidden)).T[:, 0:1]
    strip = 32
    one, zero = jnp.ones((strip, chunk), BF), jnp.zeros((strip, chunk), BF)
    base_row = iota((strip, chunk), 0).astype(F32)

    def strips(index_rows, valid_rows, length, put):
        for block in range(0, length, 256):
            rel = []
            for idx, ok in zip(index_rows, valid_rows):
                off = idx - block
                off = jnp.where(ok & (off >= 0) & (off < 256), off, -1).astype(F32)
                rel.append(jnp.broadcast_to(off, (strip, chunk)).astype(BF))
            for s in range(0, min(256, length - block), strip):
                rows = (base_row + float(s)).astype(BF)
                acc = jnp.where(rel[0] == rows, one, zero)
                for r in rel[1:]:
                    acc = acc + jnp.where(r == rows, one, zero)
                put(block + s, acc)

    cnt2 = cnt2_ref[...]

    def put2(at, value):
        counts2[at : at + strip, :] = value

    strips(
        [nbr2_ref[k : k + 1, :] for k in range(fan2)],
        [cnt2 > k for k in range(fan2)],
        mid,
        put2,
    )

    def put1(at, value):
        counts1[at : at + strip, :] = value

    def first_layer(c):
        at = pl.ds(pl.multiple_of(c * chunk, chunk), chunk)
        cnt = cnt1_ref[:, at]
        strips([nbr1_ref[k : k + 1, at] for k in range(fan1)], [cnt > k for k in range(fan1)], front, put1)
        agg = (mm(feats_t_ref[...], counts1[...]) / cnt.astype(F32)).astype(BF)
        agg_t[:, at] = agg
        z = mm(w1s_t, feats_t_ref[:, at]) + mm(w1n_t, agg) + bias
        z_t[:, at] = z
        hid_t[:, at] = (z * jax.nn.sigmoid(z)).astype(BF)

    @pl.loop(0, 1)
    def _(c):
        first_layer(c)

    for copy in asks:
        copy.wait_recv()
    asked[...] = jnp.clip(asked[...], 0, table_ref.shape[0] - 1)
    load = pltpu.make_async_copy(asked, asked_s, load_sem)
    load.start()
    load.wait()

    def gather(to, target):
        @pl.loop(0, capacity // LANES)
        def _(g):
            for j in range(LANES):
                picked[j : j + 1, :] = wide[pl.ds(asked_s[to, g, j], 1), :]
            target[to, pl.ds(pl.multiple_of(g * LANES, LANES), LANES), :] = picked[...].astype(BF)

    answers = []
    for d in order:
        to = lax.rem(feat + d, owners)
        gather(to, found)
        answers.append(
            remote(found.at[to], replies_ref.at[feat], rep_s.at[d - 1], rep_r.at[d - 1], {"feat": to})
        )
    gather(feat, replies_ref)

    @pl.loop(1, mid // chunk)
    def _(c):
        first_layer(c)

    dlog = dlog_ref[...]
    cnt2f = cnt2.astype(F32)
    agg2_t = (mm(hid_t[...], counts2[...]) / cnt2f).astype(BF)
    t2s = mm_nt(hid_t[:, 0:seeds], dlog)
    t2n = mm_nt(agg2_t, dlog)
    dself_t = mm_tn(w2s_ref[...], dlog)
    dneigh_t = mm_tn(w2n_ref[...], dlog) / cnt2f
    dn_high = dneigh_t.astype(BF)
    dn_low = (dneigh_t - dn_high.astype(F32)).astype(BF)
    t1s = jnp.zeros((width, hidden), F32)
    t1n = jnp.zeros((width, hidden), F32)
    tb1 = jnp.zeros((16, hidden), F32)
    ones = jnp.ones((16, chunk), BF)
    for c in range(0, mid, chunk):
        block = counts2[c : c + chunk, :]
        dh = mm_nt(dn_high, block) + mm_nt(dn_low, block)
        if c == 0:
            dh = dh + dself_t
        z = z_t[:, c : c + chunk]
        sig = jax.nn.sigmoid(z)
        dz = (dh * sig * (1.0 + z * (1.0 - sig))).astype(BF)
        t1s = t1s + mm_nt(feats_t_ref[:, c : c + chunk], dz)
        t1n = t1n + mm_nt(agg_t[:, c : c + chunk], dz)
        tb1 = tb1 + mm_nt(ones, dz)
    n1, n2 = width // copies, hidden // copies
    for p in range(copies):
        packed[p, 0:n1, :] = t1s[p * n1 : (p + 1) * n1].astype(BF)
        packed[p, n1 : 2 * n1, :] = t1n[p * n1 : (p + 1) * n1].astype(BF)
        two = 2 * n1
        packed[p, two : two + 2 * n2, :] = jnp.zeros((2 * n2, hidden), BF)
        packed[p, two : two + n2, 0:classes] = t2s[p * n2 : (p + 1) * n2].astype(BF)
        packed[p, two + n2 : two + 2 * n2, 0:classes] = t2n[p * n2 : (p + 1) * n2].astype(BF)
        packed[p, two + 2 * n2 :, :] = jnp.zeros((16, hidden), BF)
        packed[p, two + 2 * n2 :, 0:n2] = tb1[:, p * n2 : (p + 1) * n2].astype(BF)
    first = []
    for d in range(1, copies):
        p, where = peer(d)
        first.append(remote(packed.at[p], got.at[d - 1], s1.at[d - 1], r1.at[d - 1], where))
    total = packed[me].astype(F32)
    for d in range(1, copies):
        first[d - 1].wait_recv()
        total = total + got[d - 1].astype(F32)
    part[...] = total.astype(BF)
    second = []
    for d in order:
        second.append(
            remote(part, fed.at[feat], s2.at[d - 1], r2.at[d - 1], {"feat": lax.rem(feat + d, owners)})
        )
    fed[feat] = part[...]
    for copy in second:
        copy.wait_recv()
    total = fed[0].astype(F32)
    for f in range(1, owners):
        total = total + fed[f].astype(F32)
    out_ref[...] = (total * factor).astype(BF)
    for copy in asks + first + second + answers:
        copy.wait_send()
    for copy in answers:
        copy.wait_recv()


def run_step(owners, trainers, subs, capacity, factor, owner, row, table, feats, nbr1, cnt1, nbr2, cnt2, weights, dlog):
    w1s, w1n, bias, w2s, w2n = weights
    copies = trainers * subs
    front, width = feats.shape
    mid, seeds = nbr1.shape[0], nbr2.shape[0]
    hidden = w1s.shape[1]
    lines = front // LANES
    pages = -(-(capacity // LANES) // 8) * 8
    rows = 2 * width // copies + 2 * hidden // copies + 16
    dma = pltpu.SemaphoreType.DMA
    return pl.pallas_call(
        functools.partial(step_kernel, owners, trainers, subs, capacity, factor),
        out_shape=(
            jax.ShapeDtypeStruct((lines, LANES), jnp.int32),
            jax.ShapeDtypeStruct((owners, capacity, width), BF),
            jax.ShapeDtypeStruct((rows, hidden), BF),
        ),
        in_specs=[VM, VM, AN, AN, AN, VM, VM, VM, AN, AN, VM, VM, VM, VM],
        out_specs=(VM, VM, VM),
        scratch_shapes=[
            pltpu.VMEM(table.shape, BF),
            pltpu.VMEM(feats.shape, BF),
            pltpu.VMEM((width, front), BF),
            pltpu.VMEM((nbr1.shape[1], mid), jnp.int32),
            pltpu.VMEM(w1s.shape, BF),
            pltpu.VMEM(w1n.shape, BF),
            dma((5,)),
            pltpu.VMEM((-(-lines // 16) * 16, LANES), jnp.int32),
            pltpu.VMEM((owners, pages, LANES), jnp.int32),
            pltpu.VMEM((owners, pages, LANES), jnp.int32),
            pltpu.SMEM((owners, pages, LANES), jnp.int32),
            pltpu.VMEM(table.shape, F32),
            pltpu.VMEM((LANES, width), F32),
            pltpu.VMEM((owners, capacity, width), BF),
            pltpu.VMEM((front, seeds), BF),
            pltpu.VMEM((mid, seeds), BF),
            pltpu.VMEM((width, mid), BF),
            pltpu.VMEM((hidden, mid), F32),
            pltpu.VMEM((hidden, mid), BF),
            pltpu.VMEM((copies, rows, hidden), BF),
            pltpu.VMEM((copies - 1, rows, hidden), BF),
            pltpu.VMEM((rows, hidden), BF),
            pltpu.VMEM((owners, rows, hidden), BF),
            dma,
            dma((owners - 1,)),
            dma((owners - 1,)),
            dma((owners - 1,)),
            dma((owners - 1,)),
            dma((copies - 1,)),
            dma((copies - 1,)),
            dma((owners - 1,)),
            dma((owners - 1,)),
        ],
        compiler_params=pltpu.CompilerParams(
            collective_id=0, has_side_effects=True, vmem_limit_bytes=40 << 20
        ),
        cost_estimate=pl.CostEstimate(flops=4 << 30, bytes_accessed=60 << 20, transcendentals=1 << 20),
        name="step",
    )(
        owner.T,
        row.reshape(lines, LANES),
        table,
        feats,
        nbr1.T,
        cnt1[None, :],
        nbr2.T,
        cnt2[None, :],
        w1s,
        w1n,
        bias[None, :],
        w2s.T,
        w2n.T,
        dlog.T,
    )


def finish_kernel(slot_ref, source_ref, grads_ref, feats_ref, g1s, g1n, gb, g2s, g2n, wide, picked):
    wide[...] = source_ref[...].astype(F32)

    @pl.loop(0, slot_ref.shape[0])
    def _(g):
        for j in range(LANES):
            picked[j : j + 1, :] = wide[pl.ds(slot_ref[g, j], 1), :]
        feats_ref[pl.ds(pl.multiple_of(g * LANES, LANES), LANES), :] = picked[...].astype(BF)

    n1, n2, classes = g1s.shape[0], g2s.shape[0], g2s.shape[1]
    two = 2 * n1
    g1s[...] = grads_ref[0:n1, :]
    g1n[...] = grads_ref[n1:two, :]
    g2s[...] = grads_ref[two : two + n2, 0:classes]
    g2n[...] = grads_ref[two + n2 : two + 2 * n2, 0:classes]
    gb[...] = grads_ref[two + 2 * n2 : two + 2 * n2 + 1, 0:n2]


def finish(slot, replies, grads, n1, n2, classes):
    count = slot.shape[0] * LANES
    width, hidden = replies.shape[1], grads.shape[1]
    return pl.pallas_call(
        finish_kernel,
        out_shape=(
            jax.ShapeDtypeStruct((count, width), BF),
            jax.ShapeDtypeStruct((n1, hidden), BF),
            jax.ShapeDtypeStruct((n1, hidden), BF),
            jax.ShapeDtypeStruct((1, n2), BF),
            jax.ShapeDtypeStruct((n2, classes), BF),
            jax.ShapeDtypeStruct((n2, classes), BF),
        ),
        in_specs=[SM, VM, VM],
        out_specs=(VM,) * 6,
        scratch_shapes=[pltpu.VMEM(replies.shape, F32), pltpu.VMEM((LANES, width), F32)],
        compiler_params=pltpu.CompilerParams(vmem_limit_bytes=24 << 20),
        name="finish",
    )(slot, replies, grads)


def shards(
    trainers,
    subs,
    owners,
    table,
    cur_feats,
    nbr_first,
    cnt_first,
    nbr_second,
    cnt_second,
    w1_self,
    w1_neigh,
    bias_first,
    w2_self,
    w2_neigh,
    dlogits,
    next_owner,
    next_row,
):
    copies = trainers * subs
    front_rows, width = cur_feats.shape
    hidden, classes = w2_self.shape
    capacity = -(-(2 * front_rows // owners) // LANES) * LANES
    seeds_all = nbr_second.shape[0] * owners * copies
    slot, replies, grads = run_step(
        owners,
        trainers,
        subs,
        capacity,
        float(seeds_all) ** -0.5,
        next_owner,
        next_row,
        table,
        cur_feats,
        nbr_first,
        cnt_first,
        nbr_second,
        cnt_second,
        (w1_self, w1_neigh, bias_first, w2_self, w2_neigh),
        dlogits,
    )
    n1, n2 = width // copies, hidden // copies
    feats, g1s, g1n, gb, g2s, g2n = finish(
        slot, replies.reshape(-1, width), grads, n1, n2, classes
    )
    return feats, g1s, g1n, gb.reshape(-1), g2s, g2n


def solution(mesh):
    every = ("groups", "feat", "trainer", "sub")
    share = ("groups", "trainer", "sub")
    placed = (
        P(("groups", "feat"), None),
        P(every, None),
        P(every, None),
        P(every),
        P(every, None),
        P(every),
        P("groups", None),
        P("groups", None),
        P("groups"),
        P("groups", None),
        P("groups", None),
        P(every, None),
        P(every, None),
        P(every),
    )
    shape = mesh.shape
    return jax.shard_map(
        functools.partial(shards, shape["trainer"], shape["sub"], shape["feat"]),
        mesh=mesh,
        in_specs=placed,
        out_specs=(
            P(every, None),
            P(share, None),
            P(share, None),
            P(share),
            P(share, None),
            P(share, None),
        ),
        check_vma=False,
    )
```

```python
import functools

import jax
import jax.numpy as jnp
from jax import lax
from jax.experimental import pallas as pl
from jax.experimental.pallas import tpu as pltpu
from jax.sharding import PartitionSpec as P

BF = jnp.bfloat16
F32 = jnp.float32
VM = pl.BlockSpec(memory_space=pltpu.VMEM)
HB = pl.BlockSpec(memory_space=pltpu.HBM)
SM = pl.BlockSpec(memory_space=pltpu.SMEM)
MESH = pl.DeviceIdType.MESH
LANES = 128


def mm(left, right):
    return jnp.dot(left, right, preferred_element_type=F32)


def mm_nt(left, right):
    return lax.dot_general(left, right, (((1,), (1,)), ((), ())), preferred_element_type=F32)


def mm_tn(left, right):
    return lax.dot_general(left, right, (((0,), (0,)), ((), ())), preferred_element_type=F32)


def iota(shape, dim):
    return lax.broadcasted_iota(jnp.int32, shape, dim)


def make_requests(owners, capacity, owner_ref, row_ref, slot_ref, send_ref, own_pad):
    rows = row_ref.shape[0]
    padded = own_pad.shape[0]
    own_pad[...] = jnp.full(own_pad.shape, -1, jnp.int32)
    for r in range(rows):
        own_pad[r : r + 1, :] = owner_ref[:, r * LANES : (r + 1) * LANES]
    own = own_pad[...]
    before = (iota((LANES, LANES), 0) < iota((LANES, LANES), 1)).astype(F32).astype(BF)
    every = jnp.ones((LANES, LANES), BF)
    above = (iota((padded, padded), 0) > iota((padded, padded), 1)).astype(F32).astype(BF)
    rank = jnp.zeros(own.shape, F32)
    for o in range(owners):
        named = (own == o).astype(F32)
        named16 = named.astype(BF)
        inside = mm(named16, before)
        totals = mm(named16, every).astype(BF)
        rank = rank + named * (inside + mm(above, totals))
    slot = own * capacity + rank.astype(jnp.int32)
    slot = slot[0:rows, :]
    slot_ref[...] = slot
    row = row_ref[...]
    high, low = (row >> 6).astype(F32), (row & 63).astype(F32)
    group, place = slot >> 7, slot & 127
    each = capacity // LANES
    groups = owners * each
    total = jnp.zeros((2 * groups, LANES), F32)
    gid = iota((groups, LANES), 0)
    lid = iota((LANES, LANES), 0)
    for r in range(rows):
        hit = gid == group[r : r + 1, :]
        left = jnp.concatenate(
            [jnp.where(hit, high[r : r + 1, :], 0.0), jnp.where(hit, low[r : r + 1, :], 0.0)], axis=0
        ).astype(BF)
        right = (lid == place[r : r + 1, :]).astype(F32).astype(BF)
        total = total + mm_nt(left, right)
    asked = (total[:groups] * 64.0 + total[groups:]).astype(jnp.int32)
    send_ref[...] = jnp.zeros(send_ref.shape, jnp.int32)
    for o in range(owners):
        send_ref[o, 0:each, :] = asked[o * each : (o + 1) * each]


def step_kernel(
    owners,
    trainers,
    subs,
    capacity,
    factor,
    owner_h,
    row_h,
    table_h,
    feats_h,
    nbr1_h,
    cnt1_h,
    nbr2_h,
    cnt2_h,
    w1s_h,
    w1n_h,
    bias_h,
    w2s_ref,
    w2n_ref,
    dlog_ref,
    slot_ref,
    replies_ref,
    out_ref,
    table_ref,
    feats_v,
    feats_t_ref,
    nbr1_ref,
    w1s_ref,
    w1n_ref,
    owner_ref,
    row_ref,
    cnt1_ref,
    nbr2_ref,
    cnt2_ref,
    bias_ref,
    fetch_sem,
    own_pad,
    send,
    asked,
    asked_s,
    wide,
    picked,
    found,
    counts1,
    counts2,
    agg_t,
    z_t,
    hid_t,
    packed,
    got,
    part,
    fed,
    load_sem,
    ask_s,
    ask_r,
    rep_s,
    rep_r,
    s1,
    r1,
    s2,
    r2,
):
    copies = trainers * subs
    me = lax.axis_index("trainer") * subs + lax.axis_index("sub")
    feat = lax.axis_index("feat")

    def peer(d):
        p = lax.rem(me + d, copies)
        return p, {"trainer": p // subs, "sub": lax.rem(p, subs)}

    def remote(src, dst, send_sem, recv_sem, where):
        copy = pltpu.make_async_remote_copy(
            src_ref=src,
            dst_ref=dst,
            send_sem=send_sem,
            recv_sem=recv_sem,
            device_id=where,
            device_id_type=MESH,
        )
        copy.start()
        return copy

    fetches = []
    for n, (src, dst) in enumerate(
        (
            (owner_h, owner_ref),
            (row_h, row_ref),
            (table_h, table_ref),
            (feats_h, feats_v),
            (nbr1_h, nbr1_ref),
            (w1s_h, w1s_ref),
            (w1n_h, w1n_ref),
            (cnt1_h, cnt1_ref),
            (nbr2_h, nbr2_ref),
            (cnt2_h, cnt2_ref),
            (bias_h, bias_ref),
        )
    ):
        fetches.append(pltpu.make_async_copy(src, dst, fetch_sem.at[n]))
        fetches[-1].start()
    barrier = pltpu.get_barrier_semaphore()
    for d in range(1, copies):
        pl.semaphore_signal(barrier, inc=1, device_id=peer(d)[1], device_id_type=MESH)
    for d in range(1, owners):
        pl.semaphore_signal(
            barrier, inc=1, device_id={"feat": lax.rem(feat + d, owners)}, device_id_type=MESH
        )
    fetches[0].wait()
    fetches[1].wait()
    make_requests(owners, capacity, owner_ref, row_ref, slot_ref, send, own_pad)
    pl.semaphore_wait(barrier, copies + owners - 2)
    order = sorted(range(1, owners), key=lambda d: abs(2 * d - owners))
    asks = []
    for d in order:
        to = lax.rem(feat + d, owners)
        asks.append(
            remote(send.at[to], asked.at[feat], ask_s.at[d - 1], ask_r.at[d - 1], {"feat": to})
        )
    asked[feat] = send[feat]
    for fetch in fetches[2:]:
        fetch.wait()
    wide[...] = table_ref[...].astype(F32)
    for r in range(0, feats_v.shape[0], LANES):
        feats_t_ref[:, r : r + LANES] = feats_v[r : r + LANES, :].T

    width, front = feats_t_ref.shape
    fan1, mid = nbr1_ref.shape
    fan2, seeds = nbr2_ref.shape
    classes, hidden = w2s_ref.shape
    chunk = seeds
    w1s_t, w1n_t = w1s_ref[...].T, w1n_ref[...].T
    bias = jnp.broadcast_to(bias_ref[...], (LANES, hidden)).T[:, 0:1]
    strip = 32
    one, zero = jnp.ones((strip, chunk), BF), jnp.zeros((strip, chunk), BF)
    base_row = iota((strip, chunk), 0).astype(F32)

    def strips(index_rows, valid_rows, length, put):
        for block in range(0, length, 256):
            rel = []
            for idx, ok in zip(index_rows, valid_rows):
                off = idx - block
                off = jnp.where(ok & (off >= 0) & (off < 256), off, -1).astype(F32)
                rel.append(jnp.broadcast_to(off, (strip, chunk)).astype(BF))
            for s in range(0, min(256, length - block), strip):
                rows = (base_row + float(s)).astype(BF)
                acc = jnp.where(rel[0] == rows, one, zero)
                for r in rel[1:]:
                    acc = acc + jnp.where(r == rows, one, zero)
                put(block + s, acc)

    cnt2 = cnt2_ref[...]

    def put2(at, value):
        counts2[at : at + strip, :] = value

    strips(
        [nbr2_ref[k : k + 1, :] for k in range(fan2)],
        [cnt2 > k for k in range(fan2)],
        mid,
        put2,
    )

    def put1(at, value):
        counts1[at : at + strip, :] = value

    def first_layer(c):
        at = pl.ds(pl.multiple_of(c * chunk, chunk), chunk)
        cnt = cnt1_ref[:, at]
        strips([nbr1_ref[k : k + 1, at] for k in range(fan1)], [cnt > k for k in range(fan1)], front, put1)
        agg = (mm(feats_t_ref[...], counts1[...]) / cnt.astype(F32)).astype(BF)
        agg_t[:, at] = agg
        z = mm(w1s_t, feats_t_ref[:, at]) + mm(w1n_t, agg) + bias
        z_t[:, at] = z
        hid_t[:, at] = (z * jax.nn.sigmoid(z)).astype(BF)

    @pl.loop(0, 1)
    def _(c):
        first_layer(c)

    for copy in asks:
        copy.wait_recv()
    asked[...] = jnp.clip(asked[...], 0, table_ref.shape[0] - 1)
    load = pltpu.make_async_copy(asked, asked_s, load_sem)
    load.start()
    load.wait()

    def gather(to, target):
        @pl.loop(0, capacity // LANES)
        def _(g):
            for j in range(LANES):
                picked[j : j + 1, :] = wide[pl.ds(asked_s[to, g, j], 1), :]
            target[to, pl.ds(pl.multiple_of(g * LANES, LANES), LANES), :] = picked[...].astype(BF)

    answers = []
    for d in order:
        to = lax.rem(feat + d, owners)
        gather(to, found)
        answers.append(
            remote(found.at[to], replies_ref.at[feat], rep_s.at[d - 1], rep_r.at[d - 1], {"feat": to})
        )
    gather(feat, replies_ref)

    @pl.loop(1, mid // chunk)
    def _(c):
        first_layer(c)

    dlog = dlog_ref[...]
    cnt2f = cnt2.astype(F32)
    agg2_t = (mm(hid_t[...], counts2[...]) / cnt2f).astype(BF)
    t2s = mm_nt(hid_t[:, 0:seeds], dlog)
    t2n = mm_nt(agg2_t, dlog)
    dself_t = mm_tn(w2s_ref[...], dlog)
    dneigh_t = mm_tn(w2n_ref[...], dlog) / cnt2f
    dn_high = dneigh_t.astype(BF)
    dn_low = (dneigh_t - dn_high.astype(F32)).astype(BF)
    t1s = jnp.zeros((width, hidden), F32)
    t1n = jnp.zeros((width, hidden), F32)
    tb1 = jnp.zeros((16, hidden), F32)
    ones = jnp.ones((16, chunk), BF)
    for c in range(0, mid, chunk):
        block = counts2[c : c + chunk, :]
        dh = mm_nt(dn_high, block) + mm_nt(dn_low, block)
        if c == 0:
            dh = dh + dself_t
        z = z_t[:, c : c + chunk]
        sig = jax.nn.sigmoid(z)
        dz = (dh * sig * (1.0 + z * (1.0 - sig))).astype(BF)
        t1s = t1s + mm_nt(feats_t_ref[:, c : c + chunk], dz)
        t1n = t1n + mm_nt(agg_t[:, c : c + chunk], dz)
        tb1 = tb1 + mm_nt(ones, dz)
    n1, n2 = width // copies, hidden // copies
    for p in range(copies):
        packed[p, 0:n1, :] = t1s[p * n1 : (p + 1) * n1].astype(BF)
        packed[p, n1 : 2 * n1, :] = t1n[p * n1 : (p + 1) * n1].astype(BF)
        two = 2 * n1
        packed[p, two : two + 2 * n2, :] = jnp.zeros((2 * n2, hidden), BF)
        packed[p, two : two + n2, 0:classes] = t2s[p * n2 : (p + 1) * n2].astype(BF)
        packed[p, two + n2 : two + 2 * n2, 0:classes] = t2n[p * n2 : (p + 1) * n2].astype(BF)
        packed[p, two + 2 * n2 :, :] = jnp.zeros((16, hidden), BF)
        packed[p, two + 2 * n2 :, 0:n2] = tb1[:, p * n2 : (p + 1) * n2].astype(BF)
    first = []
    for d in range(1, copies):
        p, where = peer(d)
        first.append(remote(packed.at[p], got.at[d - 1], s1.at[d - 1], r1.at[d - 1], where))
    total = packed[me].astype(F32)
    for d in range(1, copies):
        first[d - 1].wait_recv()
        total = total + got[d - 1].astype(F32)
    part[...] = total.astype(BF)
    second = []
    for d in order:
        second.append(
            remote(part, fed.at[feat], s2.at[d - 1], r2.at[d - 1], {"feat": lax.rem(feat + d, owners)})
        )
    fed[feat] = part[...]
    for copy in second:
        copy.wait_recv()
    total = fed[0].astype(F32)
    for f in range(1, owners):
        total = total + fed[f].astype(F32)
    out_ref[...] = (total * factor).astype(BF)
    for copy in asks + first + second + answers:
        copy.wait_send()
    for copy in answers:
        copy.wait_recv()


def run_step(owners, trainers, subs, capacity, factor, owner, row, table, feats, nbr1, cnt1, nbr2, cnt2, weights, dlog):
    w1s, w1n, bias, w2s, w2n = weights
    copies = trainers * subs
    front, width = feats.shape
    mid, seeds = nbr1.shape[0], nbr2.shape[0]
    hidden = w1s.shape[1]
    lines = front // LANES
    pages = -(-(capacity // LANES) // 8) * 8
    rows = 2 * width // copies + 2 * hidden // copies + 16
    dma = pltpu.SemaphoreType.DMA
    return pl.pallas_call(
        functools.partial(step_kernel, owners, trainers, subs, capacity, factor),
        out_shape=(
            jax.ShapeDtypeStruct((lines, LANES), jnp.int32),
            jax.ShapeDtypeStruct((owners, capacity, width), BF),
            jax.ShapeDtypeStruct((rows, hidden), BF),
        ),
        in_specs=[HB] * 11 + [VM] * 3,
        out_specs=(VM, VM, VM),
        scratch_shapes=[
            pltpu.VMEM(table.shape, BF),
            pltpu.VMEM(feats.shape, BF),
            pltpu.VMEM((width, front), BF),
            pltpu.VMEM((nbr1.shape[1], mid), jnp.int32),
            pltpu.VMEM(w1s.shape, BF),
            pltpu.VMEM(w1n.shape, BF),
            pltpu.VMEM((1, front), jnp.int32),
            pltpu.VMEM((lines, LANES), jnp.int32),
            pltpu.VMEM((1, mid), jnp.int32),
            pltpu.VMEM((nbr2.shape[1], seeds), jnp.int32),
            pltpu.VMEM((1, seeds), jnp.int32),
            pltpu.VMEM((1, hidden), F32),
            dma((11,)),
            pltpu.VMEM((-(-lines // 16) * 16, LANES), jnp.int32),
            pltpu.VMEM((owners, pages, LANES), jnp.int32),
            pltpu.VMEM((owners, pages, LANES), jnp.int32),
            pltpu.SMEM((owners, pages, LANES), jnp.int32),
            pltpu.VMEM(table.shape, F32),
            pltpu.VMEM((LANES, width), F32),
            pltpu.VMEM((owners, capacity, width), BF),
            pltpu.VMEM((front, seeds), BF),
            pltpu.VMEM((mid, seeds), BF),
            pltpu.VMEM((width, mid), BF),
            pltpu.VMEM((hidden, mid), F32),
            pltpu.VMEM((hidden, mid), BF),
            pltpu.VMEM((copies, rows, hidden), BF),
            pltpu.VMEM((copies - 1, rows, hidden), BF),
            pltpu.VMEM((rows, hidden), BF),
            pltpu.VMEM((owners, rows, hidden), BF),
            dma,
            dma((owners - 1,)),
            dma((owners - 1,)),
            dma((owners - 1,)),
            dma((owners - 1,)),
            dma((copies - 1,)),
            dma((copies - 1,)),
            dma((owners - 1,)),
            dma((owners - 1,)),
        ],
        compiler_params=pltpu.CompilerParams(
            collective_id=0, has_side_effects=True, vmem_limit_bytes=61 << 20
        ),
        cost_estimate=pl.CostEstimate(flops=4 << 30, bytes_accessed=60 << 20, transcendentals=1 << 20),
        name="step",
    )(
        owner.T,
        row.reshape(lines, LANES),
        table,
        feats,
        nbr1.T,
        cnt1[None, :],
        nbr2.T,
        cnt2[None, :],
        w1s,
        w1n,
        bias[None, :],
        w2s.T,
        w2n.T,
        dlog.T,
    )


def finish_kernel(slot_ref, source_ref, grads_ref, feats_ref, g1s, g1n, gb, g2s, g2n, wide, picked):
    wide[...] = source_ref[...].astype(F32)

    @pl.loop(0, slot_ref.shape[0])
    def _(g):
        for j in range(LANES):
            picked[j : j + 1, :] = wide[pl.ds(slot_ref[g, j], 1), :]
        feats_ref[pl.ds(pl.multiple_of(g * LANES, LANES), LANES), :] = picked[...].astype(BF)

    n1, n2, classes = g1s.shape[0], g2s.shape[0], g2s.shape[1]
    two = 2 * n1
    g1s[...] = grads_ref[0:n1, :]
    g1n[...] = grads_ref[n1:two, :]
    g2s[...] = grads_ref[two : two + n2, 0:classes]
    g2n[...] = grads_ref[two + n2 : two + 2 * n2, 0:classes]
    gb[...] = grads_ref[two + 2 * n2 : two + 2 * n2 + 1, 0:n2]


def finish(slot, replies, grads, n1, n2, classes):
    count = slot.shape[0] * LANES
    width, hidden = replies.shape[1], grads.shape[1]
    return pl.pallas_call(
        finish_kernel,
        out_shape=(
            jax.ShapeDtypeStruct((count, width), BF),
            jax.ShapeDtypeStruct((n1, hidden), BF),
            jax.ShapeDtypeStruct((n1, hidden), BF),
            jax.ShapeDtypeStruct((1, n2), BF),
            jax.ShapeDtypeStruct((n2, classes), BF),
            jax.ShapeDtypeStruct((n2, classes), BF),
        ),
        in_specs=[SM, VM, VM],
        out_specs=(VM,) * 6,
        scratch_shapes=[pltpu.VMEM(replies.shape, F32), pltpu.VMEM((LANES, width), F32)],
        compiler_params=pltpu.CompilerParams(vmem_limit_bytes=61 << 20),
        name="finish",
    )(slot, replies, grads)


def shards(
    trainers,
    subs,
    owners,
    table,
    cur_feats,
    nbr_first,
    cnt_first,
    nbr_second,
    cnt_second,
    w1_self,
    w1_neigh,
    bias_first,
    w2_self,
    w2_neigh,
    dlogits,
    next_owner,
    next_row,
):
    copies = trainers * subs
    front_rows, width = cur_feats.shape
    hidden, classes = w2_self.shape
    capacity = -(-(2 * front_rows // owners) // LANES) * LANES
    seeds_all = nbr_second.shape[0] * owners * copies
    slot, replies, grads = run_step(
        owners,
        trainers,
        subs,
        capacity,
        float(seeds_all) ** -0.5,
        next_owner,
        next_row,
        table,
        cur_feats,
        nbr_first,
        cnt_first,
        nbr_second,
        cnt_second,
        (w1_self, w1_neigh, bias_first, w2_self, w2_neigh),
        dlogits,
    )
    n1, n2 = width // copies, hidden // copies
    feats, g1s, g1n, gb, g2s, g2n = finish(
        slot, replies.reshape(-1, width), grads, n1, n2, classes
    )
    return feats, g1s, g1n, gb.reshape(-1), g2s, g2n


def solution(mesh):
    every = ("groups", "feat", "trainer", "sub")
    share = ("groups", "trainer", "sub")
    placed = (
        P(("groups", "feat"), None),
        P(every, None),
        P(every, None),
        P(every),
        P(every, None),
        P(every),
        P("groups", None),
        P("groups", None),
        P("groups"),
        P("groups", None),
        P("groups", None),
        P(every, None),
        P(every, None),
        P(every),
    )
    shape = mesh.shape
    return jax.shard_map(
        functools.partial(shards, shape["trainer"], shape["sub"], shape["feat"]),
        mesh=mesh,
        in_specs=placed,
        out_specs=(
            P(every, None),
            P(share, None),
            P(share, None),
            P(share),
            P(share, None),
            P(share, None),
        ),
        check_vma=False,
    )
```
